32 devices in a mesh: crop: 2 (over x), row: 16 (over z, y, core).
Axes of the slice: x: 2, y: 2, z: 4, core: 2. Of those that a mesh axis runs over, the one named last changes fastest.
Arguments:
- pair_input: bfloat16 [256, 128, 128], P(('crop', 'row')), parts along dimension 0, may hold values from -52 to 52
- residue_mask: int32 [256], P('crop'), parts along dimension 0, may hold values from 0 to 1, as said below
- outgoing_norm: bfloat16 [128], replicated, may hold values from 0.5 to 1.5
- outgoing_proj: bfloat16 [128, 512], replicated, may hold values from -0.5 to 0.5
- outgoing_gate: bfloat16 [128, 128], replicated, may hold values from -0.5 to 0.5
- outgoing_scale: bfloat16 [128], replicated, may hold values from 0.5 to 1.5
- outgoing_output: bfloat16 [128, 128], replicated, may hold values from -0.5 to 0.5
- incoming_norm: bfloat16 [128], replicated, may hold values from 0.5 to 1.5
- incoming_proj: bfloat16 [128, 512], replicated, may hold values from -0.5 to 0.5
- incoming_gate: bfloat16 [128, 128], replicated, may hold values from -0.5 to 0.5
- incoming_scale: bfloat16 [128], replicated, may hold values from 0.5 to 1.5
- incoming_output: bfloat16 [128, 128], replicated, may hold values from -0.5 to 0.5
- attention_norm: bfloat16 [128], replicated, may hold values from 0.5 to 1.5
- query_weight: bfloat16 [128, 128], replicated, may hold values from -1.2 to 1.2
- key_weight: bfloat16 [128, 128], replicated, may hold values from -1.2 to 1.2
- value_weight: bfloat16 [128, 128], replicated, may hold values from -0.5 to 0.5
- bias_weight: bfloat16 [128, 4], replicated, may hold values from -0.5 to 0.5
- attention_gate: bfloat16 [128, 128], replicated, may hold values from -0.5 to 0.5
- attention_output: bfloat16 [128, 128], replicated, may hold values from -0.5 to 0.5
Outputs:
- updated_pair: float32 [256, 128, 128], P(('crop', 'row')), parts along dimension 0
The draws below stay inside these ranges and needn't reach their ends.
There are 2 independent parts, one for each index of `crop`. The reference program is written for one: setup_inputs(seed, part) draws one part's arguments, and reference() takes and returns one part's arrays. A program takes and returns all parts, laid end to end along the dimension named above; an argument that names none is the same for every part. Nothing has to cross between parts.
Inputs may be any that keep to these rules, and one draw needn't show every extreme that they name: residue_mask is 1 on a prefix of at least 64 residues and 0 after it.
All inputs are finite; a program needn't handle non-finite values.
Results may differ from the reference program's by a relative error of at most 0.013.
Values may be sent and summed in bfloat16 or wider, within the bound.
A program may use at most 64 MiB of HBM per device.

```python
import math
import jax
import jax.numpy as jnp
from jax import lax

C = 128
HID = 128
H = 4
HD = 32
N = 128


def projection_draw(key):
    base_draw = jnp.clip(jax.random.normal(key, (C, H * HD), jnp.float32), -4.0, 4.0) * C ** (-0.5)
    return base_draw.astype(jnp.bfloat16)


def draw_query_weight(key, part):
    key = jax.random.fold_in(key, 11)
    return projection_draw(key)


def draw_key_weight(key, part):
    key = jax.random.fold_in(key, 13)
    return projection_draw(key)


def draw_pair_input(key, part):
    key = jax.random.fold_in(key, 3)
    subkeys = jax.random.split(key, 3)
    chan_scale = jnp.exp(jax.random.uniform(subkeys[0], (C,), jnp.float32, math.log(0.3), math.log(3.0)))
    pos_scale = jnp.exp(jax.random.uniform(subkeys[1], (N, N, 1), jnp.float32, math.log(0.5), math.log(2.0)))
    noise = jnp.clip(jax.random.normal(subkeys[2], (N, N, C), jnp.float32), -4.0, 4.0)
    values = noise * chan_scale * pos_scale
    return values.astype(jnp.bfloat16)


def draw_residue_mask(key, part):
    key = jax.random.fold_in(key, 7)
    length = jax.random.randint(key, (), N // 2, N + 1)
    return (jnp.arange(N, dtype=jnp.int32) < length).astype(jnp.int32)


def centred(own_key, shape, scale, reach, kind=jnp.bfloat16):
    drawn = scale * jax.random.normal(own_key, shape, jnp.float32)
    return jnp.clip(drawn, min=-reach, max=reach).astype(kind)


def setup_inputs(seed: int = 0, part: int = 0) -> dict:
    arg_keys = jax.random.split(jax.random.key(seed), 20)
    part_splits = jax.random.split(jax.random.fold_in(arg_keys[19], part), 20)
    pair_input = draw_pair_input(jax.random.fold_in(jax.random.fold_in(arg_keys[19], part), 71), part)
    residue_mask = draw_residue_mask(jax.random.fold_in(jax.random.fold_in(arg_keys[19], part), 71), part)
    outgoing_norm = jnp.clip(1.0 + 0.1 * jax.random.normal(arg_keys[2], (C,), jnp.float32), 0.5, 1.5).astype(jnp.bfloat16)
    outgoing_proj = centred(arg_keys[3], (C, 4 * HID), C ** -0.5, 0.5)
    outgoing_gate = centred(arg_keys[4], (C, C), C ** -0.5, 0.5)
    outgoing_scale = jnp.clip(1.0 + 0.1 * jax.random.normal(arg_keys[5], (HID,), jnp.float32), 0.5, 1.5).astype(jnp.bfloat16)
    outgoing_output = centred(arg_keys[6], (HID, C), HID ** -0.5, 0.5)
    incoming_norm = jnp.clip(1.0 + 0.1 * jax.random.normal(arg_keys[7], (C,), jnp.float32), 0.5, 1.5).astype(jnp.bfloat16)
    incoming_proj = centred(arg_keys[8], (C, 4 * HID), C ** -0.5, 0.5)
    incoming_gate = centred(arg_keys[9], (C, C), C ** -0.5, 0.5)
    incoming_scale = jnp.clip(1.0 + 0.1 * jax.random.normal(arg_keys[10], (HID,), jnp.float32), 0.5, 1.5).astype(jnp.bfloat16)
    incoming_output = centred(arg_keys[11], (HID, C), HID ** -0.5, 0.5)
    attention_norm = jnp.clip(1.0 + 0.1 * jax.random.normal(arg_keys[12], (C,), jnp.float32), 0.5, 1.5).astype(jnp.bfloat16)
    query_weight = draw_query_weight(jax.random.fold_in(arg_keys[19], 71), part)
    key_weight = draw_key_weight(jax.random.fold_in(arg_keys[19], 71), part)
    value_weight = centred(arg_keys[15], (C, H * HD), C ** -0.5, 0.5)
    bias_weight = centred(arg_keys[16], (C, H), C ** -0.5, 0.5)
    attention_gate = centred(arg_keys[17], (C, H * HD), C ** -0.5, 0.5)
    attention_output = centred(arg_keys[18], (H * HD, C), (H * HD) ** -0.5, 0.5)
    return dict(pair_input=pair_input, residue_mask=residue_mask, outgoing_norm=outgoing_norm, outgoing_proj=outgoing_proj, outgoing_gate=outgoing_gate, outgoing_scale=outgoing_scale, outgoing_output=outgoing_output, incoming_norm=incoming_norm, incoming_proj=incoming_proj, incoming_gate=incoming_gate, incoming_scale=incoming_scale, incoming_output=incoming_output, attention_norm=attention_norm, query_weight=query_weight, key_weight=key_weight, value_weight=value_weight, bias_weight=bias_weight, attention_gate=attention_gate, attention_output=attention_output)


EPSILON = 1e-05

def layer_norm(values, gain, axis):
    values = values.astype(jnp.float32)
    centre = values - lax.optimization_barrier(jnp.mean(values, axis=axis, keepdims=True))
    spread = lax.optimization_barrier(jnp.mean(centre * centre, axis=axis, keepdims=True))
    return centre * lax.rsqrt(spread + EPSILON) * gain

def triangle(pair_state, pair_mask, norm_gain, projection, gate_weight, tri_gain, output_weight, incoming):
    hidden = tri_gain.shape[0]
    normed = layer_norm(pair_state, norm_gain.astype(jnp.float32), -1).astype(jnp.bfloat16)
    normed_full = normed.astype(jnp.float32)
    projected = jnp.einsum('ijc,cd->ijd', normed_full, projection.astype(jnp.float32))
    masking = pair_mask[:, :, None]
    left_side = (jax.nn.sigmoid(projected[..., hidden:2 * hidden]) * projected[..., :hidden] * masking).astype(jnp.bfloat16)
    right_side = (jax.nn.sigmoid(projected[..., 3 * hidden:]) * projected[..., 2 * hidden:3 * hidden] * masking).astype(jnp.bfloat16)
    left_side = lax.optimization_barrier(left_side).astype(jnp.float32)
    right_side = lax.optimization_barrier(right_side).astype(jnp.float32)
    if incoming:
        product = jnp.einsum('kic,kjc->ijc', left_side, right_side)
    else:
        product = jnp.einsum('ikc,jkc->ijc', left_side, right_side)
    product = product.astype(jnp.bfloat16)
    tri_normed = layer_norm(product, tri_gain.astype(jnp.float32), -1).astype(jnp.bfloat16)
    gating = jax.nn.sigmoid(jnp.einsum('ijc,cd->ijd', normed_full, gate_weight.astype(jnp.float32)))
    update = jnp.einsum('ijh,hc->ijc', tri_normed.astype(jnp.float32), output_weight.astype(jnp.float32))
    return (pair_state.astype(jnp.float32) + gating * update).astype(jnp.bfloat16)

def attention(pair_state, col_mask, norm_gain, query_weight, key_weight, value_weight, bias_weight, gate_weight, output_weight):
    normed = layer_norm(pair_state, norm_gain.astype(jnp.float32), -1).astype(jnp.bfloat16)
    normed_full = normed.astype(jnp.float32)
    score_scale = HD ** (-0.5)
    query_proj = (jnp.einsum('ijc,cd->ijd', normed_full, query_weight.astype(jnp.float32)) * score_scale).astype(jnp.bfloat16)
    key_proj = jnp.einsum('ijc,cd->ijd', normed_full, key_weight.astype(jnp.float32)).astype(jnp.bfloat16)
    value_proj = jnp.einsum('ijc,cd->ijd', normed_full, value_weight.astype(jnp.float32)).astype(jnp.bfloat16)
    bias_full = jnp.einsum('jkc,ch->hjk', normed_full, bias_weight.astype(jnp.float32)).astype(jnp.bfloat16)
    bias_full = lax.optimization_barrier(bias_full).astype(jnp.float32)
    gating = jax.nn.sigmoid(jnp.einsum('ijc,cd->ijd', normed_full, gate_weight.astype(jnp.float32)))
    key_penalty = 1000000000.0 * (col_mask - 1.0)

    def single_row(row_index):
        query_block = query_proj[row_index].astype(jnp.float32).reshape(N, H, HD)
        key_block = key_proj[row_index].astype(jnp.float32).reshape(N, H, HD)
        value_block = value_proj[row_index].astype(jnp.float32).reshape(N, H, HD)
        scores = jnp.einsum('jhd,khd->hjk', query_block, key_block) + bias_full + key_penalty
        scores = scores - lax.optimization_barrier(jnp.max(scores, axis=2, keepdims=True))
        weights = jnp.exp(scores)
        weights = (weights / lax.optimization_barrier(jnp.sum(weights, axis=2, keepdims=True))).astype(jnp.bfloat16)
        weights = lax.optimization_barrier(weights).astype(jnp.float32)
        return jnp.einsum('hjk,khd->jhd', weights, value_block).reshape(N, H * HD)
    head_out = lax.map(single_row, jnp.arange(N, dtype=jnp.int32))
    gated = (gating * head_out).astype(jnp.bfloat16)
    gated = lax.optimization_barrier(gated).astype(jnp.float32)
    update = jnp.einsum('ijd,dc->ijc', gated, output_weight.astype(jnp.float32))
    return pair_state.astype(jnp.float32) + update

def reference(pair_input, residue_mask, outgoing_norm, outgoing_proj, outgoing_gate, outgoing_scale, outgoing_output, incoming_norm, incoming_proj, incoming_gate, incoming_scale, incoming_output, attention_norm, query_weight, key_weight, value_weight, bias_weight, attention_gate, attention_output):
    col_mask = residue_mask.astype(jnp.float32)
    pair_mask = col_mask[:, None] * col_mask[None, :]
    first_pass = triangle(pair_input, pair_mask, outgoing_norm, outgoing_proj, outgoing_gate, outgoing_scale, outgoing_output, False)
    second_pass = triangle(first_pass, pair_mask, incoming_norm, incoming_proj, incoming_gate, incoming_scale, incoming_output, True)
    return attention(second_pass, col_mask, attention_norm, query_weight, key_weight, value_weight, bias_weight, attention_gate, attention_output)
```

```python
import functools

import jax
import jax.numpy as jnp
from jax import lax
from jax.experimental import pallas as pl
from jax.experimental.pallas import tpu as pltpu
from jax.sharding import PartitionSpec as P

EPSILON = 1e-05
F32 = jnp.float32
BF16 = jnp.bfloat16
LANES = 128
TRI = ("norm", "proj", "gate", "scale", "output")


def dot(a, b):
    return lax.dot_general(a, b, (((1,), (0,)), ((), ())), preferred_element_type=F32)


def flip(a):
    return jnp.transpose(a.astype(F32))


def sigmoid(a):
    return 1.0 / (1.0 + jnp.exp(-a))


def kernel(
    n_dev,
    x_ref,
    mask_ref,
    mask_smem,
    *refs,
):
    weights, rest = refs[:17], refs[17:]
    out_ref = rest[0]
    (
        pair,
        normed,
        gates,
        turned,
        spread_out,
        wt,
        gain,
        send_l,
        send_r,
        recv_l,
        recv_r,
        send_t,
        recv_t,
        send_b,
        recv_b,
        bias_t,
        q_buf,
        k_buf,
        v_buf,
        send_sem,
        recv_sem,
    ) = rest[1:]
    tri_weights = (weights[0:5], weights[5:10])
    att_norm, wq, wk, wv, wb, wag, wao = weights[10:17]
    rows, cols, chans = x_ref.shape
    heads = wb.shape[1]
    head_size = wq.shape[1] // heads
    scale = head_size ** (-0.5)
    own = chans // n_dev * rows
    me = lax.axis_index("row")
    blocks = cols // LANES
    single = cols <= 128

    barrier = pltpu.get_barrier_semaphore()

    def greet(step, carry):
        pl.semaphore_signal(
            barrier, inc=1, device_id={"row": lax.rem(me + step, n_dev)}, device_id_type=pl.DeviceIdType.MESH
        )
        return carry

    lax.fori_loop(1, n_dev, greet, 0)

    def each_row(body):
        if single:
            for r in range(rows):
                body(r)
        else:
            def step(r, carry):
                body(r)
                return carry
            lax.fori_loop(0, rows, step, 0)

    def copy(phase, step, src, dst):
        return pltpu.make_async_remote_copy(
            src_ref=src,
            dst_ref=dst,
            send_sem=send_sem.at[phase, step],
            recv_sem=recv_sem.at[phase, step],
            device_id={"row": lax.rem(me + step, n_dev)},
            device_id_type=pl.DeviceIdType.MESH,
        )

    def span(d):
        return pl.ds(pl.multiple_of(d * own, 16), own)

    plans = {}
    for t in range(2):
        plans[3 * t] = (lambda d, t=t: send_l.at[t, span(d), :], lambda d, t=t: recv_l.at[t, d])
        plans[3 * t + 1] = (lambda d, t=t: send_r.at[t, span(d), :], lambda d, t=t: recv_r.at[t, d])
        plans[3 * t + 2] = (lambda d, t=t: send_t.at[t, d], lambda d, t=t: recv_t.at[t, span(d), :])
    plans[6] = (lambda d: send_b, lambda d: recv_b.at[d])

    def send(phase):
        src, dst = plans[phase]

        def step(s, carry):
            copy(phase, s, src(lax.rem(me + s, n_dev)), dst(me)).start()
            return carry

        lax.fori_loop(1, n_dev, step, 0)

    def await_recv(phase):
        src, dst = plans[phase]

        def step(s, carry):
            sender = lax.rem(me - s + n_dev, n_dev)
            copy(phase, s, src(sender), dst(sender)).wait_recv()
            return carry

        lax.fori_loop(1, n_dev, step, 0)

    def await_send(phase):
        src, dst = plans[phase]

        def step(s, carry):
            copy(phase, s, src(lax.rem(me + s, n_dev)), dst(me)).wait_send()
            return carry

        lax.fori_loop(1, n_dev, step, 0)

    def wide(column):
        return column if single else jnp.concatenate([column] * blocks, axis=1)

    def column(vec_ref):
        row = vec_ref[...].astype(F32)
        return jnp.transpose(jnp.broadcast_to(row, (LANES, LANES)))

    def norm(values, gain_column):
        centre = values - jnp.mean(values, axis=0, keepdims=True)
        spread = jnp.mean(centre * centre, axis=0, keepdims=True)
        return centre * lax.rsqrt(spread + EPSILON) * wide(gain_column)

    def put_row(r, value):
        for b in range(blocks):
            spread_out[b, pl.ds(r, chans, stride=rows), :] = value[:, b * LANES : (b + 1) * LANES]

    def get_row(r):
        parts = [spread_out[b, pl.ds(r, chans, stride=rows), :] for b in range(blocks)]
        return parts[0] if single else jnp.concatenate(parts, axis=1)

    col_mask = mask_ref[...].astype(F32)

    def turn(slot, ref, count):
        for b in range(count):
            wt[slot + b] = flip(ref[:, b * LANES : (b + 1) * LANES]).astype(BF16)

    def turn_triangle(t):
        gain[0] = column(tri_weights[t][0])
        gain[1] = column(tri_weights[t][3])
        turn(0, tri_weights[t][1], 4)
        turn(4, tri_weights[t][2], 1)
        turn(5, tri_weights[t][4], 1)

    def load(r):
        pair[r] = flip(x_ref[r])

    def triangle(t):
        def normalise(r):
            normed[r] = norm(pair[r], gain[0]).astype(BF16)

        each_row(normalise)

        def operand(first, send_buf):
            def one(r):
                val = dot(wt[first], normed[r])
                logit = dot(wt[first + 1], normed[r])
                present = mask_smem[me * rows + r].astype(F32) * col_mask
                put_row(r, sigmoid(logit) * val * present)

            each_row(one)
            for b in range(blocks):
                send_buf[t, :, b * LANES : (b + 1) * LANES] = spread_out[b].astype(BF16)

        operand(0, send_l)
        if t == 0:
            pl.semaphore_wait(barrier, n_dev - 1)
        send(3 * t)
        operand(2, send_r)
        send(3 * t + 1)
        recv_l[t, me] = send_l[t, span(me), :]
        recv_r[t, me] = send_r[t, span(me), :]

        def gate(r):
            gates[r] = sigmoid(dot(wt[4], normed[r]))

        each_row(gate)
        await_recv(3 * t)
        await_recv(3 * t + 1)

        for c in range(0, own // rows, 2):
            both = []
            for k in range(2):
                pick = pl.ds(c * rows, 2 * rows)
                take = lambda ref: (
                    ref[t, :, pick, :].astype(F32)[:, k * rows : (k + 1) * rows, :].reshape(cols, cols).astype(BF16)
                )
                left, right = take(recv_l), take(recv_r)
                dims = ((0,), (0,)) if t else ((1,), (1,))
                tri = lax.dot_general(left, right, (dims, ((), ())), preferred_element_type=F32)
                both.append(tri.reshape(n_dev, rows, cols))
            send_t[t, :, pl.ds(c * rows, 2 * rows), :] = jnp.concatenate(both, axis=1).astype(BF16)
        send(3 * t + 2)
        recv_t[t, span(me), :] = send_t[t, me]
        await_recv(3 * t + 2)

        for b in range(blocks):
            lane = slice(b * LANES, (b + 1) * LANES)
            values = recv_t[t, :, lane].astype(F32).reshape(chans, rows, LANES)
            centre = values - jnp.mean(values, axis=0, keepdims=True)
            spread = jnp.mean(centre * centre, axis=0, keepdims=True)
            spread_out[b] = (centre * lax.rsqrt(spread + EPSILON)).reshape(chans * rows, LANES)

        def update(r):
            tri_normed = (get_row(r) * wide(gain[1])).astype(BF16)
            change = dot(wt[5], tri_normed)
            pair[r] = (pair[r] + gates[r] * change).astype(BF16).astype(F32)

        each_row(update)

    turn_triangle(0)
    each_row(load)
    triangle(0)
    turn_triangle(1)
    triangle(1)

    gain[0] = column(att_norm)
    for slot, ref in enumerate((wq, wv, wag, wao)):
        turn(slot, ref, 1)
    bias_w = flip(wb[...]).astype(BF16)

    def bias(r):
        value = norm(pair[r], gain[0])
        normed[r] = value.astype(BF16)
        local = dot(bias_w, normed[r])
        for b in range(blocks):
            spread_out[b, pl.ds(r, heads, stride=rows), :] = local[:, b * LANES : (b + 1) * LANES]

    each_row(bias)
    for b in range(blocks):
        send_b[:, b * LANES : (b + 1) * LANES] = spread_out[b, : heads * rows, :].astype(BF16)
    send(6)
    recv_b[me] = send_b[...]

    def project(r):
        flat = normed[r]
        q_buf[r] = (dot(wt[0], flat) * scale).astype(BF16)
        k_buf[r] = dot(flip(flat).astype(BF16), wk[...]).astype(BF16)
        v_buf[r] = dot(wt[1], flat).astype(BF16)
        gates[r] = sigmoid(dot(wt[2], flat))

    each_row(project)
    await_recv(6)
    penalty = 1000000000.0 * (col_mask - 1.0)
    every = recv_b[...].astype(F32)
    for h in range(heads):
        one = every[:, h * rows : (h + 1) * rows, :].reshape(cols, cols) + penalty
        bias_t[h] = jnp.transpose(one)

    def attend(r):
        outs = []
        for h in range(heads):
            part = slice(h * head_size, (h + 1) * head_size)
            pieces = []
            if h:
                pieces.append(jnp.zeros((h * head_size, cols), BF16))
            pieces.append(q_buf[r, part, :])
            if h < heads - 1:
                pieces.append(jnp.zeros(((heads - 1 - h) * head_size, cols), BF16))
            scores = dot(k_buf[r], jnp.concatenate(pieces, axis=0)) + bias_t[h]
            scores = jnp.exp(scores - jnp.max(scores, axis=0, keepdims=True))
            total = jnp.sum(scores, axis=0, keepdims=True)
            outs.append(dot(v_buf[r, part, :], scores.astype(BF16)) / total)
        gated = (gates[r] * jnp.concatenate(outs, axis=0)).astype(BF16)
        out_ref[r] = jnp.transpose(pair[r] + dot(wt[3], gated))

    each_row(attend)
    for phase in range(7):
        await_send(phase)


def shards(n_dev, pair_input, residue_mask, *weights):
    rows, cols, chans = pair_input.shape
    heads = weights[14].shape[1]
    own = chans // n_dev * rows
    weights = [w.reshape(1, -1) if w.ndim == 1 else w for w in weights]
    vmem = pl.BlockSpec(memory_space=pltpu.VMEM)
    v = pltpu.VMEM
    return pl.pallas_call(
        functools.partial(kernel, n_dev),
        out_shape=jax.ShapeDtypeStruct((rows, cols, chans), F32),
        in_specs=[vmem, vmem, pl.BlockSpec(memory_space=pltpu.SMEM)] + [vmem] * len(weights),
        out_specs=vmem,
        scratch_shapes=[
            v((rows, chans, cols), F32),
            v((rows, chans, cols), BF16),
            v((rows, chans, cols), F32),
            v((8, LANES), F32),
            v((cols // LANES, chans * rows, LANES), F32),
            v((6, chans, chans), BF16),
            v((2, chans, LANES), F32),
            v((2, chans * rows, cols), BF16),
            v((2, chans * rows, cols), BF16),
            v((2, n_dev, own, cols), BF16),
            v((2, n_dev, own, cols), BF16),
            v((2, n_dev, own, cols), BF16),
            v((2, chans * rows, cols), BF16),
            v((heads * rows, cols), BF16),
            v((n_dev, heads * rows, cols), BF16),
            v((heads, cols, cols), F32),
            v((rows, chans, cols), BF16),
            v((rows, cols, chans), BF16),
            v((rows, chans, cols), BF16),
            pltpu.SemaphoreType.DMA((7, n_dev)),
            pltpu.SemaphoreType.DMA((7, n_dev)),
        ],
        compiler_params=pltpu.CompilerParams(
            collective_id=0, has_side_effects=True, vmem_limit_bytes=56 * 1024 * 1024
        ),
    )(pair_input, residue_mask.reshape(1, -1), residue_mask, *weights)


def solution(mesh):
    return jax.shard_map(
        functools.partial(shards, mesh.shape["row"]),
        mesh=mesh,
        in_specs=(P(("crop", "row"), None, None), P("crop")) + (P(),) * 17,
        out_specs=P(("crop", "row"), None, None),
        check_vma=False,
    )
```

```python
import functools

import jax
import jax.numpy as jnp
from jax import lax
from jax.experimental import pallas as pl
from jax.experimental.pallas import tpu as pltpu
from jax.sharding import PartitionSpec as P

EPSILON = 1e-05
F32 = jnp.float32
BF16 = jnp.bfloat16
LANES = 128


def layout(n_dev, rows, chans, t):
    group = n_dev if t else n_dev // 2
    own = chans // group * rows
    return group, own, 2 if own % 32 == 0 else 1


def dot(a, b):
    return lax.dot_general(a, b, (((1,), (0,)), ((), ())), preferred_element_type=F32)


def flip(a):
    return jnp.transpose(a.astype(F32))


def sigmoid(a):
    return 1.0 / (1.0 + jnp.exp(-a))


def kernel(
    n_dev,
    x_ref,
    mask_ref,
    mask_smem,
    *refs,
):
    weights, rest = refs[:17], refs[17:]
    out_ref = rest[0]
    (
        pair,
        normed,
        gates,
        spread_out,
        wt,
        gain,
        send_l,
        send_r,
        recv_l0,
        recv_l1,
        recv_r0,
        recv_r1,
        send_t0,
        send_t1,
        recv_t,
        send_b,
        recv_b,
        bias_t,
        q_buf,
        k_buf,
        v_buf,
        send_sem,
        recv_sem,
    ) = rest[1:]
    tri_weights = (weights[0:5], weights[5:10])
    att_norm, wq, wk, wv, wb, wag, wao = weights[10:17]
    rows, cols, chans = x_ref.shape
    heads = wb.shape[0]
    head_size = wq.shape[1] // heads
    scale = head_size ** (-0.5)
    recv_l, recv_r, send_t = (recv_l0, recv_l1), (recv_r0, recv_r1), (send_t0, send_t1)
    me = lax.axis_index("row")
    blocks = cols // LANES
    single = cols <= 128

    barrier = pltpu.get_barrier_semaphore()

    def greet(step, carry):
        pl.semaphore_signal(
            barrier, inc=1, device_id={"row": lax.rem(me + step, n_dev)}, device_id_type=pl.DeviceIdType.MESH
        )
        return carry

    lax.fori_loop(1, n_dev, greet, 0)

    def each_row(body):
        if single:
            for r in range(rows):
                body(r)
        else:
            def step(r, carry):
                body(r)
                return carry
            lax.fori_loop(0, rows, step, 0)

    group, own, parts, here, base = [], [], [], [], []
    for t in range(2):
        size, block, cuts = layout(n_dev, rows, chans, t)
        group.append(size)
        own.append(block)
        parts.append(cuts)
        here.append(lax.rem(me, size))
        base.append(me - lax.rem(me, size))

    def aligned(start, size):
        return pl.ds(pl.multiple_of(start, 16), size)

    def span(t, d):
        return aligned(d * own[t], own[t])

    def piece(t, k, d=None):
        size = own[t] // parts[t]
        return pl.ds(k * size, size) if d is None else aligned(d * own[t] + k * size, size)

    plans = {}
    for t in range(2):
        ring = (group[t], base[t], here[t])
        whole = (n_dev, 0, me)
        plans["l", t, 0] = ring + (
            lambda d, t=t: send_l.at[t, span(t, d), :],
            lambda d, t=t: recv_l[t].at[d],
        )
        for k in range(parts[t]):
            plans["r", t, k] = whole + (
                lambda d, t=t, k=k: send_r.at[t, piece(t, k, lax.rem(d, group[t])), :],
                lambda d, t=t, k=k: recv_r[t].at[d, piece(t, k), :],
            )
            plans["t", t, k] = ring + (
                lambda d, t=t, k=k: send_t[t].at[d, piece(t, k), :],
                lambda d, t=t, k=k: recv_t.at[t, piece(t, k, d), :],
            )
    plans["b", 2, 0] = (n_dev, 0, me, lambda d: send_b, lambda d: recv_b.at[d])
    numbers = {key: number for number, key in enumerate(plans)}

    def copy(key, step, src, dst):
        size, first, place = plans[key][:3]
        return pltpu.make_async_remote_copy(
            src_ref=src,
            dst_ref=dst,
            send_sem=send_sem.at[numbers[key], step],
            recv_sem=recv_sem.at[numbers[key], step],
            device_id={"row": first + lax.rem(place + step, size)},
            device_id_type=pl.DeviceIdType.MESH,
        )

    def send(*key):
        size, _, place, src, dst = plans[key]

        def step(s, carry):
            copy(key, s, src(lax.rem(place + s, size)), dst(place)).start()
            return carry

        lax.fori_loop(1, size, step, 0)

    def await_recv(*key):
        size, _, place, src, dst = plans[key]

        def step(s, carry):
            sender = lax.rem(place - s + size, size)
            copy(key, s, src(sender), dst(sender)).wait_recv()
            return carry

        lax.fori_loop(1, size, step, 0)

    def await_send(*key):
        size, _, place, src, dst = plans[key]

        def step(s, carry):
            copy(key, s, src(lax.rem(place + s, size)), dst(place)).wait_send()
            return carry

        lax.fori_loop(1, size, step, 0)

    def wide(column):
        return column if single else jnp.concatenate([column] * blocks, axis=1)

    def column(vec_ref):
        row = vec_ref[...].astype(F32)
        return jnp.transpose(jnp.broadcast_to(row, (LANES, LANES)))

    def norm(values, gain_column):
        centre = values - jnp.mean(values, axis=0, keepdims=True)
        spread = jnp.mean(centre * centre, axis=0, keepdims=True)
        return centre * lax.rsqrt(spread + EPSILON) * wide(gain_column)

    def put_row(r, value):
        for b in range(blocks):
            spread_out[b, pl.ds(r, chans, stride=rows), :] = value[:, b * LANES : (b + 1) * LANES]

    def get_row(r):
        parts = [spread_out[b, pl.ds(r, chans, stride=rows), :] for b in range(blocks)]
        return parts[0] if single else jnp.concatenate(parts, axis=1)

    col_mask = mask_ref[...].astype(F32)

    def turn(t, slot, ref, count):
        for b in range(count):
            wt[t, slot + b] = flip(ref[:, b * LANES : (b + 1) * LANES]).astype(BF16)

    def turn_triangle(t):
        gain[t, 0] = column(tri_weights[t][0])
        gain[t, 1] = column(tri_weights[t][3])
        turn(t, 0, tri_weights[t][1], 4)
        turn(t, 4, tri_weights[t][2], 1)
        turn(t, 5, tri_weights[t][4], 1)

    def load(r):
        pair[r] = flip(x_ref[r])

    def triangle(t, between):
        def normalise(r):
            normed[r] = norm(pair[r], gain[t, 0]).astype(BF16)

        each_row(normalise)

        def operand(first, send_buf):
            def one(r):
                val = dot(wt[t, first], normed[r])
                logit = dot(wt[t, first + 1], normed[r])
                present = mask_smem[me * rows + r].astype(F32) * col_mask
                put_row(r, sigmoid(logit) * val * present)

            each_row(one)
            for b in range(blocks):
                send_buf[t, :, b * LANES : (b + 1) * LANES] = spread_out[b].astype(BF16)

        operand(2, send_r)
        if t == 0:
            pl.semaphore_wait(barrier, n_dev - 1)
        send("r", t, 0)
        operand(0, send_l)
        send("l", t, 0)
        for k in range(1, parts[t]):
            send("r", t, k)
        recv_l[t][here[t]] = send_l[t, span(t, here[t])]
        recv_r[t][me] = send_r[t, span(t, here[t])]

        def gate(r):
            gates[r] = sigmoid(dot(wt[t, 4], normed[r]))

        each_row(gate)
        between()
        await_recv("l", t, 0)
        dims = ((0,), (0,)) if t else ((1,), (1,))
        for k in range(parts[t]):
            await_recv("r", t, k)
            size = own[t] // parts[t]
            for start in range(k * size, (k + 1) * size, 2 * rows):
                pick = pl.ds(start, 2 * rows)
                left = recv_l[t][:, pick, :].astype(F32)
                right = recv_r[t][:, pick, :].astype(F32)
                both = []
                for c in range(2):
                    take = lambda values: (
                        values[:, c * rows : (c + 1) * rows, :].reshape(-1, cols).astype(BF16)
                    )
                    tri = lax.dot_general(take(left), take(right), (dims, ((), ())), preferred_element_type=F32)
                    both.append(tri.reshape(group[t], rows, cols))
                send_t[t][:, pick, :] = jnp.concatenate(both, axis=1).astype(BF16)
            send("t", t, k)
        recv_t[t, span(t, here[t]), :] = send_t[t][here[t]]
        for k in range(parts[t]):
            await_recv("t", t, k)

        for b in range(blocks):
            lane = slice(b * LANES, (b + 1) * LANES)
            values = recv_t[t, :, lane].astype(F32).reshape(chans, rows, LANES)
            centre = values - jnp.mean(values, axis=0, keepdims=True)
            spread = jnp.mean(centre * centre, axis=0, keepdims=True)
            spread_out[b] = (centre * lax.rsqrt(spread + EPSILON)).reshape(chans * rows, LANES)

        def update(r):
            tri_normed = (get_row(r) * wide(gain[t, 1])).astype(BF16)
            change = dot(wt[t, 5], tri_normed)
            pair[r] = (pair[r] + gates[r] * change).astype(BF16).astype(F32)

        each_row(update)

    def turn_attention():
        gain[2, 0] = column(att_norm)
        for slot, ref in enumerate((wq, wv, wag, wao)):
            turn(2, slot, ref, 1)

    turn_triangle(0)
    each_row(load)
    triangle(0, lambda: turn_triangle(1))
    triangle(1, turn_attention)
    bias_w = wb[...]

    def bias(r):
        value = norm(pair[r], gain[2, 0])
        normed[r] = value.astype(BF16)
        local = dot(bias_w, normed[r])
        for b in range(blocks):
            spread_out[b, pl.ds(r, heads, stride=rows), :] = local[:, b * LANES : (b + 1) * LANES]

    each_row(bias)
    for b in range(blocks):
        send_b[:, b * LANES : (b + 1) * LANES] = spread_out[b, : heads * rows, :].astype(BF16)
    send("b", 2, 0)
    recv_b[me] = send_b[...]

    def project(r):
        flat = normed[r]
        q_buf[r] = (dot(wt[2, 0], flat) * scale).astype(BF16)
        k_buf[r] = dot(flip(flat).astype(BF16), wk[...]).astype(BF16)
        v_buf[r] = dot(wt[2, 1], flat).astype(BF16)
        gates[r] = sigmoid(dot(wt[2, 2], flat))

    each_row(project)
    await_recv("b", 2, 0)
    penalty = 1000000000.0 * (col_mask - 1.0)
    every = recv_b[...].astype(F32)
    for h in range(heads):
        one = every[:, h * rows : (h + 1) * rows, :].reshape(cols, cols) + penalty
        bias_t[h] = jnp.transpose(one)

    def attend(r):
        outs = []
        for h in range(heads):
            part = slice(h * head_size, (h + 1) * head_size)
            pieces = []
            if h:
                pieces.append(jnp.zeros((h * head_size, cols), BF16))
            pieces.append(q_buf[r, part, :])
            if h < heads - 1:
                pieces.append(jnp.zeros(((heads - 1 - h) * head_size, cols), BF16))
            scores = dot(k_buf[r], jnp.concatenate(pieces, axis=0)) + bias_t[h]
            scores = jnp.exp(scores - jnp.max(scores, axis=0, keepdims=True))
            total = jnp.sum(scores, axis=0, keepdims=True)
            outs.append(dot(v_buf[r, part, :], scores.astype(BF16)) / total)
        gated = (gates[r] * jnp.concatenate(outs, axis=0)).astype(BF16)
        out_ref[r] = jnp.transpose(pair[r] + dot(wt[2, 3], gated))

    each_row(attend)
    for key in plans:
        await_send(*key)


def shards(n_dev, pair_input, residue_mask, *weights):
    rows, cols, chans = pair_input.shape
    heads = weights[14].shape[1]
    group0, own0, parts0 = layout(n_dev, rows, chans, 0)
    group1, own1, parts1 = layout(n_dev, rows, chans, 1)
    phases = 3 + 2 * parts0 + 2 * parts1
    weights = list(weights)
    weights[14] = weights[14].T
    weights = [w.reshape(1, -1) if w.ndim == 1 else w for w in weights]
    vmem = pl.BlockSpec(memory_space=pltpu.VMEM)
    v = pltpu.VMEM
    return pl.pallas_call(
        functools.partial(kernel, n_dev),
        out_shape=jax.ShapeDtypeStruct((rows, cols, chans), F32),
        in_specs=[vmem, vmem, pl.BlockSpec(memory_space=pltpu.SMEM)] + [vmem] * len(weights),
        out_specs=vmem,
        scratch_shapes=[
            v((rows, chans, cols), F32),
            v((rows, chans, cols), BF16),
            v((rows, chans, cols), F32),
            v((cols // LANES, chans * rows, LANES), F32),
            v((3, 6, chans, chans), BF16),
            v((3, 2, chans, LANES), F32),
            v((2, chans * rows, cols), BF16),
            v((2, chans * rows, cols), BF16),
            v((group0, own0, cols), BF16),
            v((group1, own1, cols), BF16),
            v((n_dev, own0, cols), BF16),
            v((n_dev, own1, cols), BF16),
            v((group0, own0, cols), BF16),
            v((group1, own1, cols), BF16),
            v((2, chans * rows, cols), BF16),
            v((heads * rows, cols), BF16),
            v((n_dev, heads * rows, cols), BF16),
            v((heads, cols, cols), F32),
            v((rows, chans, cols), BF16),
            v((rows, cols, chans), BF16),
            v((rows, chans, cols), BF16),
            pltpu.SemaphoreType.DMA((phases, n_dev)),
            pltpu.SemaphoreType.DMA((phases, n_dev)),
        ],
        compiler_params=pltpu.CompilerParams(
            collective_id=0, has_side_effects=True, vmem_limit_bytes=56 * 1024 * 1024
        ),
    )(pair_input, residue_mask.reshape(1, -1), residue_mask, *weights)


def solution(mesh):
    return jax.shard_map(
        functools.partial(shards, mesh.shape["row"]),
        mesh=mesh,
        in_specs=(P(("crop", "row"), None, None), P("crop")) + (P(),) * 17,
        out_specs=P(("crop", "row"), None, None),
        check_vma=False,
    )
```

```python
import functools

import jax
import jax.numpy as jnp
from jax import lax
from jax.experimental import pallas as pl
from jax.experimental.pallas import tpu as pltpu
from jax.sharding import PartitionSpec as P

EPSILON = 1e-05
F32 = jnp.float32
BF16 = jnp.bfloat16
LANES = 128


def layout(n_dev, rows, chans, t):
    group = n_dev if t else n_dev // 2
    own = chans // group * rows
    return group, own, 2 if own % 32 == 0 else 1


def dot(a, b):
    return lax.dot_general(a, b, (((1,), (0,)), ((), ())), preferred_element_type=F32)


def flip(a):
    return jnp.transpose(a.astype(F32))


def sigmoid(a):
    return 0.5 * jnp.tanh(0.5 * a) + 0.5


def kernel(
    n_dev,
    x_hbm,
    mask_ref,
    mask_smem,
    *refs,
):
    weights_hbm, out_hbm, rest = refs[:17], refs[17], refs[17:]
    (
        pair,
        normed,
        gates,
        spread_out,
        wt,
        gain,
        send_l,
        send_r,
        recv_l0,
        recv_l1,
        recv_r0,
        recv_r1,
        send_t0,
        send_t1,
        recv_t,
        send_b,
        recv_b,
        bias_t,
        q_buf,
        k_buf,
        v_buf,
        early,
        out_ref,
        send_sem,
        recv_sem,
        load_sem,
        store_sem,
        x_ref,
        *weights,
    ) = rest[1:]
    loads = [
        pltpu.make_async_copy(src, dst, load_sem.at[i])
        for i, (src, dst) in enumerate(zip((x_hbm, *weights_hbm), (x_ref, *weights)))
    ]
    for i in (0, 1, 2, *range(3, len(loads))):
        loads[i].start()

    def need(*operands):
        for i in operands:
            loads[1 + i].wait()

    tri_weights = (weights[0:5], weights[5:10])
    att_norm, wq, wk, wv, wb, wag, wao = weights[10:17]
    rows, cols, chans = x_ref.shape
    heads = wb.shape[0]
    head_size = wq.shape[1] // heads
    scale = head_size ** (-0.5)
    recv_l, recv_r, send_t = (recv_l0, recv_l1), (recv_r0, recv_r1), (send_t0, send_t1)
    me = lax.axis_index("row")
    blocks = cols // LANES
    single = cols <= 128

    barrier = pltpu.get_barrier_semaphore()

    def greet(step, carry):
        pl.semaphore_signal(
            barrier, inc=1, device_id={"row": lax.rem(me + step, n_dev)}, device_id_type=pl.DeviceIdType.MESH
        )
        return carry

    lax.fori_loop(1, n_dev, greet, 0)

    def each_row(body):
        if single:
            for r in range(rows):
                body(r)
        else:
            def step(r, carry):
                body(r)
                return carry
            lax.fori_loop(0, rows, step, 0)

    group, own, parts, here, base = [], [], [], [], []
    for t in range(2):
        size, block, cuts = layout(n_dev, rows, chans, t)
        group.append(size)
        own.append(block)
        parts.append(cuts)
        here.append(lax.rem(me, size))
        base.append(me - lax.rem(me, size))

    def aligned(start, size):
        return pl.ds(pl.multiple_of(start, 16), size)

    def span(t, d):
        return aligned(d * own[t], own[t])

    def piece(t, k, d=None):
        size = own[t] // parts[t]
        return pl.ds(k * size, size) if d is None else aligned(d * own[t] + k * size, size)

    plans = {}
    for t in range(2):
        ring = (group[t], base[t], here[t])
        whole = (n_dev, 0, me)
        plans["l", t, 0] = ring + (
            lambda d, t=t: send_l.at[t, span(t, d), :],
            lambda d, t=t: recv_l[t].at[d],
        )
        for k in range(parts[t]):
            plans["r", t, k] = whole + (
                lambda d, t=t, k=k: send_r.at[t, piece(t, k, lax.rem(d, group[t])), :],
                lambda d, t=t, k=k: recv_r[t].at[d, piece(t, k), :],
            )
            plans["t", t, k] = ring + (
                lambda d, t=t, k=k: send_t[t].at[d, piece(t, k), :],
                lambda d, t=t, k=k: recv_t.at[t, piece(t, k, d), :],
            )
    plans["b", 2, 0] = (n_dev, 0, me, lambda d: send_b, lambda d: recv_b.at[d])
    numbers = {key: number for number, key in enumerate(plans)}

    def copy(key, step, src, dst):
        size, first, place = plans[key][:3]
        return pltpu.make_async_remote_copy(
            src_ref=src,
            dst_ref=dst,
            send_sem=send_sem.at[numbers[key], step],
            recv_sem=recv_sem.at[numbers[key], step],
            device_id={"row": first + lax.rem(place + step, size)},
            device_id_type=pl.DeviceIdType.MESH,
        )

    def send(*key):
        size, _, place, src, dst = plans[key]

        def step(s, carry):
            copy(key, s, src(lax.rem(place + s, size)), dst(place)).start()
            return carry

        lax.fori_loop(1, size, step, 0)

    def await_recv(*key):
        size, _, place, src, dst = plans[key]

        def step(s, carry):
            sender = lax.rem(place - s + size, size)
            copy(key, s, src(sender), dst(sender)).wait_recv()
            return carry

        lax.fori_loop(1, size, step, 0)

    def await_send(*key):
        size, _, place, src, dst = plans[key]

        def step(s, carry):
            copy(key, s, src(lax.rem(place + s, size)), dst(place)).wait_send()
            return carry

        lax.fori_loop(1, size, step, 0)

    def wide(column):
        return column if single else jnp.concatenate([column] * blocks, axis=1)

    def column(vec_ref):
        row = vec_ref[...].astype(F32)
        return jnp.transpose(jnp.broadcast_to(row, (LANES, LANES)))

    def norm(values, gain_column):
        centre = values - jnp.mean(values, axis=0, keepdims=True)
        spread = jnp.mean(centre * centre, axis=0, keepdims=True)
        return centre * lax.rsqrt(spread + EPSILON) * wide(gain_column)

    def put_row(r, value):
        for b in range(blocks):
            spread_out[b, pl.ds(r, chans, stride=rows), :] = value[:, b * LANES : (b + 1) * LANES]

    def get_row(r):
        parts = [spread_out[b, pl.ds(r, chans, stride=rows), :] for b in range(blocks)]
        return parts[0] if single else jnp.concatenate(parts, axis=1)

    col_mask = mask_ref[...].astype(F32)

    def turn(t, slot, ref, count):
        for b in range(count):
            wt[t, slot + b] = flip(ref[:, b * LANES : (b + 1) * LANES]).astype(BF16)

    def turn_first(t):
        need(5 * t, 5 * t + 1)
        gain[t, 0] = column(tri_weights[t][0])
        for b in (2, 3, 0, 1):
            wt[t, b] = flip(tri_weights[t][1][:, b * chans : (b + 1) * chans]).astype(BF16)

    def turn_second(t):
        need(5 * t + 2, 5 * t + 3, 5 * t + 4)
        gain[t, 1] = column(tri_weights[t][3])
        turn(t, 4, tri_weights[t][2], 1)
        turn(t, 5, tri_weights[t][4], 1)

    def load(r):
        pair[r] = flip(x_ref[r])

    def triangle(t, between):
        def normalise(r):
            normed[r] = norm(pair[r], gain[t, 0]).astype(BF16)

        each_row(normalise)

        def operand(first, send_buf):
            def one(r):
                both = dot(wt[t, first : first + 2].reshape(2 * chans, chans), normed[r])
                val, logit = both[:chans], both[chans:]
                present = mask_smem[me * rows + r].astype(F32) * col_mask
                put_row(r, sigmoid(logit) * val * present)

            each_row(one)
            for b in range(blocks):
                send_buf[t, :, b * LANES : (b + 1) * LANES] = spread_out[b].astype(BF16)

        operand(2, send_r)
        if t == 0:
            pl.semaphore_wait(barrier, n_dev - 1)
        send("r", t, 0)
        operand(0, send_l)
        send("l", t, 0)
        recv_l[t][here[t]] = send_l[t, span(t, here[t])]
        recv_r[t][me] = send_r[t, span(t, here[t])]

        turn_second(t)

        def gate(r):
            gates[r] = sigmoid(dot(wt[t, 4], normed[r]))

        each_row(gate)
        await_recv("r", t, 0)
        for k in range(1, parts[t]):
            send("r", t, k)
        between()
        await_recv("l", t, 0)
        dims = ((0,), (0,)) if t else ((1,), (1,))
        for k in range(parts[t]):
            if k:
                await_recv("r", t, k)
            size = own[t] // parts[t]
            for start in range(k * size, (k + 1) * size, 2 * rows):
                pick = pl.ds(start, 2 * rows)
                left = recv_l[t][:, pick, :].astype(F32)
                right = recv_r[t][:, pick, :].astype(F32)
                both = []
                for c in range(2):
                    take = lambda values: (
                        values[:, c * rows : (c + 1) * rows, :].reshape(-1, cols).astype(BF16)
                    )
                    tri = lax.dot_general(take(left), take(right), (dims, ((), ())), preferred_element_type=F32)
                    both.append(tri.reshape(group[t], rows, cols))
                send_t[t][:, pick, :] = jnp.concatenate(both, axis=1).astype(BF16)
            send("t", t, k)
        recv_t[t, span(t, here[t]), :] = send_t[t][here[t]]
        for k in range(parts[t]):
            await_recv("t", t, k)

        for b in range(blocks):
            lane = slice(b * LANES, (b + 1) * LANES)
            values = recv_t[t, :, lane].astype(F32).reshape(chans, rows, LANES)
            centre = values - jnp.mean(values, axis=0, keepdims=True)
            spread = jnp.mean(centre * centre, axis=0, keepdims=True)
            spread_out[b] = (centre * lax.rsqrt(spread + EPSILON)).reshape(chans * rows, LANES)

        def update(r):
            tri_normed = (get_row(r) * wide(gain[t, 1])).astype(BF16)
            change = dot(wt[t, 5], tri_normed)
            pair[r] = (pair[r] + gates[r] * change).astype(BF16).astype(F32)

        each_row(update)

    def turn_attention():
        gain[2, 0] = column(att_norm)
        for slot, ref in enumerate((wq, wv, wag, wao)):
            turn(2, slot, ref, 1)

    def turn_attention():
        need(*range(10, 17))
        gain[2, 0] = column(att_norm)
        for slot, ref in enumerate((wq, wv, wag, wao)):
            turn(2, slot, ref, 1)

    loads[0].wait()
    each_row(load)
    turn_first(0)
    triangle(0, lambda: turn_first(1))
    triangle(1, turn_attention)
    bias_w = wb[...]

    def bias(r):
        value = norm(pair[r], gain[2, 0])
        normed[r] = value.astype(BF16)
        local = dot(bias_w, normed[r])
        for b in range(blocks):
            spread_out[b, pl.ds(r, heads, stride=rows), :] = local[:, b * LANES : (b + 1) * LANES]

    each_row(bias)
    for b in range(blocks):
        send_b[:, b * LANES : (b + 1) * LANES] = spread_out[b, : heads * rows, :].astype(BF16)
    send("b", 2, 0)
    recv_b[me] = send_b[...]

    def scores_of(r, h):
        pieces = []
        if h:
            pieces.append(jnp.zeros((h * head_size, cols), BF16))
        pieces.append(q_buf[r, h * head_size : (h + 1) * head_size, :])
        if h < heads - 1:
            pieces.append(jnp.zeros(((heads - 1 - h) * head_size, cols), BF16))
        return dot(k_buf[r], jnp.concatenate(pieces, axis=0))

    def project(r):
        flat = normed[r]
        q_buf[r] = (dot(wt[2, 0], flat) * scale).astype(BF16)
        k_buf[r] = dot(flip(flat).astype(BF16), wk[...]).astype(BF16)
        v_buf[r] = dot(wt[2, 1], flat).astype(BF16)
        gates[r] = sigmoid(dot(wt[2, 2], flat))
        if single:
            for h in range(heads):
                early[r, h] = scores_of(r, h)

    each_row(project)
    await_recv("b", 2, 0)
    penalty = 1000000000.0 * (col_mask - 1.0)
    every = recv_b[...].astype(F32)
    for h in range(heads):
        one = every[:, h * rows : (h + 1) * rows, :].reshape(cols, cols) + penalty
        bias_t[h] = jnp.transpose(one)

    def store(r):
        return pltpu.make_async_copy(out_ref.at[r], out_hbm.at[r], store_sem.at[r])

    def attend(r):
        outs = []
        for h in range(heads):
            part = slice(h * head_size, (h + 1) * head_size)
            scores = (early[r, h] if single else scores_of(r, h)) + bias_t[h]
            scores = jnp.exp(scores - jnp.max(scores, axis=0, keepdims=True))
            total = jnp.sum(scores, axis=0, keepdims=True)
            outs.append(dot(v_buf[r, part, :], scores.astype(BF16)) / total)
        gated = (gates[r] * jnp.concatenate(outs, axis=0)).astype(BF16)
        out_ref[r] = jnp.transpose(pair[r] + dot(wt[2, 3], gated))
        store(r).start()

    each_row(attend)
    for key in plans:
        await_send(*key)
    each_row(lambda r: store(r).wait())


def shards(n_dev, pair_input, residue_mask, *weights):
    rows, cols, chans = pair_input.shape
    heads = weights[14].shape[1]
    group0, own0, parts0 = layout(n_dev, rows, chans, 0)
    group1, own1, parts1 = layout(n_dev, rows, chans, 1)
    phases = 3 + 2 * parts0 + 2 * parts1
    weights = list(weights)
    weights[14] = weights[14].T
    weights = [w.reshape(1, -1) if w.ndim == 1 else w for w in weights]
    vmem = pl.BlockSpec(memory_space=pltpu.VMEM)
    hbm = pl.BlockSpec(memory_space=pl.ANY)
    v = pltpu.VMEM
    early = (rows, heads, cols, cols) if cols <= 128 else (1, 1, 8, LANES)
    return pl.pallas_call(
        functools.partial(kernel, n_dev),
        out_shape=jax.ShapeDtypeStruct((rows, cols, chans), F32),
        in_specs=[hbm, vmem, pl.BlockSpec(memory_space=pltpu.SMEM)] + [hbm] * len(weights),
        out_specs=hbm,
        scratch_shapes=[
            v((rows, chans, cols), F32),
            v((rows, chans, cols), BF16),
            v((rows, chans, cols), F32),
            v((cols // LANES, chans * rows, LANES), F32),
            v((3, 6, chans, chans), BF16),
            v((3, 2, chans, LANES), F32),
            v((2, chans * rows, cols), BF16),
            v((2, chans * rows, cols), BF16),
            v((group0, own0, cols), BF16),
            v((group1, own1, cols), BF16),
            v((n_dev, own0, cols), BF16),
            v((n_dev, own1, cols), BF16),
            v((group0, own0, cols), BF16),
            v((group1, own1, cols), BF16),
            v((2, chans * rows, cols), BF16),
            v((heads * rows, cols), BF16),
            v((n_dev, heads * rows, cols), BF16),
            v((heads, cols, cols), F32),
            v((rows, chans, cols), BF16),
            v((rows, cols, chans), BF16),
            v((rows, chans, cols), BF16),
            v(early, F32),
            v((rows, cols, chans), F32),
            pltpu.SemaphoreType.DMA((phases, n_dev)),
            pltpu.SemaphoreType.DMA((phases, n_dev)),
            pltpu.SemaphoreType.DMA((1 + len(weights),)),
            pltpu.SemaphoreType.DMA((rows,)),
            v((rows, cols, chans), BF16),
            *[v(w.shape, w.dtype) for w in weights],
        ],
        compiler_params=pltpu.CompilerParams(
            collective_id=0, has_side_effects=True, vmem_limit_bytes=56 * 1024 * 1024
        ),
    )(pair_input, residue_mask.reshape(1, -1), residue_mask, *weights)


def solution(mesh):
    return jax.shard_map(
        functools.partial(shards, mesh.shape["row"]),
        mesh=mesh,
        in_specs=(P(("crop", "row"), None, None), P("crop")) + (P(),) * 17,
        out_specs=P(("crop", "row"), None, None),
        check_vma=False,
    )
```

```python
import functools

import jax
import jax.numpy as jnp
from jax import lax
from jax.experimental import pallas as pl
from jax.experimental.pallas import tpu as pltpu
from jax.sharding import PartitionSpec as P

EPSILON = 1e-05
F32 = jnp.float32
BF16 = jnp.bfloat16
LANES = 128


def layout(n_dev, rows, chans, t):
    group = n_dev if t else n_dev // 2
    own = chans // group * rows
    return group, own, 1


def dot(a, b):
    return lax.dot_general(a, b, (((1,), (0,)), ((), ())), preferred_element_type=F32)


def wrap(a, size):
    return jnp.where(a >= size, a - size, a)


def flip(a):
    return jnp.transpose(a.astype(F32))


def sigmoid(a):
    return 0.5 * jnp.tanh(0.5 * a) + 0.5


def kernel(
    n_dev,
    x_hbm,
    mask_ref,
    mask_smem,
    *refs,
):
    weights_hbm, out_hbm, rest = refs[:17], refs[17], refs[17:]
    (
        pair,
        normed,
        gates,
        spread_out,
        wt,
        gain,
        send_l,
        send_r,
        recv_l0,
        recv_l1,
        recv_r0,
        recv_r1,
        send_t0,
        send_t1,
        recv_t,
        send_b,
        recv_b,
        bias_t,
        q_buf,
        k_buf,
        v_buf,
        early,
        out_ref,
        send_sem,
        recv_sem,
        load_sem,
        store_sem,
        x_ref,
        *weights,
    ) = rest[1:]
    loads = [
        pltpu.make_async_copy(src, dst, load_sem.at[i])
        for i, (src, dst) in enumerate(zip((x_hbm, *weights_hbm), (x_ref, *weights)))
    ]
    for i in (0, 1, 2, *range(3, len(loads))):
        loads[i].start()

    def need(*operands):
        for i in operands:
            loads[1 + i].wait()

    tri_weights = (weights[0:5], weights[5:10])
    att_norm, wq, wk, wv, wb, wag, wao = weights[10:17]
    rows, cols, chans = x_ref.shape
    heads = wb.shape[0]
    head_size = wq.shape[1] // heads
    scale = head_size ** (-0.5)
    recv_l, recv_r, send_t = (recv_l0, recv_l1), (recv_r0, recv_r1), (send_t0, send_t1)
    me = lax.axis_index("row")
    blocks = cols // LANES
    single = cols <= 128

    barrier = pltpu.get_barrier_semaphore()

    def greet(step, carry):
        pl.semaphore_signal(
            barrier, inc=1, device_id={"row": wrap(me + step, n_dev)}, device_id_type=pl.DeviceIdType.MESH
        )
        return carry

    lax.fori_loop(1, n_dev, greet, 0)

    def each_row(body):
        if single:
            for r in range(rows):
                body(r)
        else:
            def step(r, carry):
                body(r)
                return carry
            lax.fori_loop(0, rows, step, 0)

    group, own, parts, here, base = [], [], [], [], []
    for t in range(2):
        size, block, cuts = layout(n_dev, rows, chans, t)
        group.append(size)
        own.append(block)
        parts.append(cuts)
        here.append(lax.rem(me, size))
        base.append(me - lax.rem(me, size))

    def aligned(start, size):
        return pl.ds(pl.multiple_of(start, 16), size)

    def span(t, d):
        return aligned(d * own[t], own[t])

    def piece(t, k, d=None):
        size = own[t] // parts[t]
        return pl.ds(k * size, size) if d is None else aligned(d * own[t] + k * size, size)

    plans = {}
    for t in range(2):
        ring = (group[t], base[t], here[t])
        whole = (n_dev, 0, me)
        plans["l", t, 0] = ring + (
            lambda d, t=t: send_l.at[t, span(t, d), :],
            lambda d, t=t: recv_l[t].at[d],
        )
        for k in range(parts[t]):
            plans["r", t, k] = whole + (
                lambda d, t=t, k=k: send_r.at[t, piece(t, k, wrap(d, group[t])), :],
                lambda d, t=t, k=k: recv_r[t].at[d, piece(t, k), :],
            )
            plans["t", t, k] = ring + (
                lambda d, t=t, k=k: send_t[t].at[d, piece(t, k), :],
                lambda d, t=t, k=k: recv_t.at[t, piece(t, k, d), :],
            )
    plans["b", 2, 0] = (n_dev, 0, me, lambda d: send_b, lambda d: recv_b.at[d])
    numbers = {key: number for number, key in enumerate(plans)}

    def copy(key, step, src, dst):
        size, first, place = plans[key][:3]
        return pltpu.make_async_remote_copy(
            src_ref=src,
            dst_ref=dst,
            send_sem=send_sem.at[numbers[key], step],
            recv_sem=recv_sem.at[numbers[key], step],
            device_id={"row": first + wrap(place + step, size)},
            device_id_type=pl.DeviceIdType.MESH,
        )

    def send(*key):
        size, _, place, src, dst = plans[key]

        def step(s, carry):
            copy(key, s, src(wrap(place + s, size)), dst(place)).start()
            return carry

        lax.fori_loop(1, size, step, 0)

    def await_recv(*key):
        size, _, place, src, dst = plans[key]

        def step(s, carry):
            sender = wrap(place - s + size, size)
            copy(key, s, src(sender), dst(sender)).wait_recv()
            return carry

        lax.fori_loop(1, size, step, 0)

    def await_send(*key):
        size, _, place, src, dst = plans[key]

        def step(s, carry):
            copy(key, s, src(wrap(place + s, size)), dst(place)).wait_send()
            return carry

        lax.fori_loop(1, size, step, 0)

    def wide(column):
        return column if single else jnp.concatenate([column] * blocks, axis=1)

    def column(vec_ref):
        row = vec_ref[...].astype(F32)
        return jnp.transpose(jnp.broadcast_to(row, (LANES, LANES)))

    def norm(values, gain_column):
        centre = values - jnp.mean(values, axis=0, keepdims=True)
        spread = jnp.mean(centre * centre, axis=0, keepdims=True)
        return centre * lax.rsqrt(spread + EPSILON) * wide(gain_column)

    def put_row(r, value):
        for b in range(blocks):
            spread_out[b, pl.ds(r, chans, stride=rows), :] = value[:, b * LANES : (b + 1) * LANES]

    def get_row(r):
        parts = [spread_out[b, pl.ds(r, chans, stride=rows), :] for b in range(blocks)]
        return parts[0] if single else jnp.concatenate(parts, axis=1)

    col_mask = mask_ref[...].astype(F32)

    def turn(t, slot, ref, count):
        for b in range(count):
            wt[t, slot + b] = flip(ref[:, b * LANES : (b + 1) * LANES]).astype(BF16)

    def turn_first(t):
        need(5 * t, 5 * t + 1)
        gain[t, 0] = column(tri_weights[t][0])
        for b in (2, 3, 0, 1):
            wt[t, b] = flip(tri_weights[t][1][:, b * chans : (b + 1) * chans]).astype(BF16)

    def turn_second(t):
        need(5 * t + 2, 5 * t + 3, 5 * t + 4)
        gain[t, 1] = column(tri_weights[t][3])
        turn(t, 4, tri_weights[t][2], 1)
        turn(t, 5, tri_weights[t][4], 1)

    def load(r):
        pair[r] = flip(x_ref[r])

    def triangle(t, between):
        def normalise(r):
            normed[r] = norm(pair[r], gain[t, 0]).astype(BF16)

        each_row(normalise)

        def operand(first, send_buf):
            def one(r):
                both = dot(wt[t, first : first + 2].reshape(2 * chans, chans), normed[r])
                val, logit = both[:chans], both[chans:]
                present = mask_smem[me * rows + r].astype(F32) * col_mask
                put_row(r, sigmoid(logit) * val * present)

            each_row(one)
            for b in range(blocks):
                send_buf[t, :, b * LANES : (b + 1) * LANES] = spread_out[b].astype(BF16)

        operand(2, send_r)
        if t == 0:
            pl.semaphore_wait(barrier, n_dev - 1)
        send("r", t, 0)
        operand(0, send_l)
        send("l", t, 0)
        for k in range(1, parts[t]):
            send("r", t, k)
        recv_l[t][here[t]] = send_l[t, span(t, here[t])]
        recv_r[t][me] = send_r[t, span(t, here[t])]

        turn_second(t)

        def gate(r):
            gates[r] = sigmoid(dot(wt[t, 4], normed[r]))

        each_row(gate)
        await_recv("r", t, 0)
        between()
        await_recv("l", t, 0)
        dims = ((0,), (0,)) if t else ((1,), (1,))
        for k in range(parts[t]):
            if k:
                await_recv("r", t, k)
            size = own[t] // parts[t]
            for start in range(k * size, (k + 1) * size, 2 * rows):
                pick = pl.ds(start, 2 * rows)
                left = recv_l[t][:, pick, :].astype(F32)
                right = recv_r[t][:, pick, :].astype(F32)
                both = []
                for c in range(2):
                    take = lambda values: (
                        values[:, c * rows : (c + 1) * rows, :].reshape(-1, cols).astype(BF16)
                    )
                    tri = lax.dot_general(take(left), take(right), (dims, ((), ())), preferred_element_type=F32)
                    both.append(tri.reshape(group[t], rows, cols))
                send_t[t][:, pick, :] = jnp.concatenate(both, axis=1).astype(BF16)
            send("t", t, k)
        recv_t[t, span(t, here[t]), :] = send_t[t][here[t]]
        for k in range(parts[t]):
            await_recv("t", t, k)

        for b in range(blocks):
            lane = slice(b * LANES, (b + 1) * LANES)
            values = recv_t[t, :, lane].astype(F32).reshape(chans, rows, LANES)
            centre = values - jnp.mean(values, axis=0, keepdims=True)
            spread = jnp.mean(centre * centre, axis=0, keepdims=True)
            spread_out[b] = (centre * lax.rsqrt(spread + EPSILON)).reshape(chans * rows, LANES)

        def update(r):
            tri_normed = (get_row(r) * wide(gain[t, 1])).astype(BF16)
            change = dot(wt[t, 5], tri_normed)
            pair[r] = (pair[r] + gates[r] * change).astype(BF16).astype(F32)

        each_row(update)

    def turn_attention():
        gain[2, 0] = column(att_norm)
        for slot, ref in enumerate((wq, wv, wag, wao)):
            turn(2, slot, ref, 1)

    def turn_attention():
        need(*range(10, 17))
        gain[2, 0] = column(att_norm)
        for slot, ref in enumerate((wq, wv, wag, wao)):
            turn(2, slot, ref, 1)

    loads[0].wait()
    each_row(load)
    turn_first(0)
    triangle(0, lambda: turn_first(1))
    triangle(1, turn_attention)
    bias_w = wb[...]

    def bias(r):
        value = norm(pair[r], gain[2, 0])
        normed[r] = value.astype(BF16)
        local = dot(bias_w, normed[r])
        for b in range(blocks):
            spread_out[b, pl.ds(r, heads, stride=rows), :] = local[:, b * LANES : (b + 1) * LANES]

    each_row(bias)
    for b in range(blocks):
        send_b[:, b * LANES : (b + 1) * LANES] = spread_out[b, : heads * rows, :].astype(BF16)
    send("b", 2, 0)
    recv_b[me] = send_b[...]

    def scores_of(r, h):
        pieces = []
        if h:
            pieces.append(jnp.zeros((h * head_size, cols), BF16))
        pieces.append(q_buf[r, h * head_size : (h + 1) * head_size, :])
        if h < heads - 1:
            pieces.append(jnp.zeros(((heads - 1 - h) * head_size, cols), BF16))
        return dot(k_buf[r], jnp.concatenate(pieces, axis=0))

    def project(r):
        flat = normed[r]
        q_buf[r] = (dot(wt[2, 0], flat) * scale).astype(BF16)
        k_buf[r] = dot(flip(flat).astype(BF16), wk[...]).astype(BF16)
        v_buf[r] = dot(wt[2, 1], flat).astype(BF16)
        gates[r] = sigmoid(dot(wt[2, 2], flat))
        if single:
            for h in range(heads):
                early[r, h] = scores_of(r, h)

    each_row(project)
    await_recv("b", 2, 0)
    penalty = 1000000000.0 * (col_mask - 1.0)
    every = recv_b[...].astype(F32)
    for h in range(heads):
        one = every[:, h * rows : (h + 1) * rows, :].reshape(cols, cols) + penalty
        bias_t[h] = jnp.transpose(one)

    def store(r):
        return pltpu.make_async_copy(out_ref.at[r], out_hbm.at[r], store_sem.at[r])

    def attend(r):
        outs = []
        for h in range(heads):
            part = slice(h * head_size, (h + 1) * head_size)
            scores = (early[r, h] if single else scores_of(r, h)) + bias_t[h]
            scores = jnp.exp(scores - jnp.max(scores, axis=0, keepdims=True))
            total = jnp.sum(scores, axis=0, keepdims=True)
            outs.append(dot(v_buf[r, part, :], scores.astype(BF16)) / total)
        gated = (gates[r] * jnp.concatenate(outs, axis=0)).astype(BF16)
        out_ref[r] = jnp.transpose(pair[r] + dot(wt[2, 3], gated))
        store(r).start()

    each_row(attend)
    for key in plans:
        await_send(*key)
    each_row(lambda r: store(r).wait())


def shards(n_dev, pair_input, residue_mask, *weights):
    rows, cols, chans = pair_input.shape
    heads = weights[14].shape[1]
    group0, own0, parts0 = layout(n_dev, rows, chans, 0)
    group1, own1, parts1 = layout(n_dev, rows, chans, 1)
    phases = 3 + 2 * parts0 + 2 * parts1
    weights = list(weights)
    weights[14] = weights[14].T
    weights = [w.reshape(1, -1) if w.ndim == 1 else w for w in weights]
    vmem = pl.BlockSpec(memory_space=pltpu.VMEM)
    hbm = pl.BlockSpec(memory_space=pl.ANY)
    v = pltpu.VMEM
    early = (rows, heads, cols, cols) if cols <= 128 else (1, 1, 8, LANES)
    return pl.pallas_call(
        functools.partial(kernel, n_dev),
        out_shape=jax.ShapeDtypeStruct((rows, cols, chans), F32),
        in_specs=[hbm, vmem, pl.BlockSpec(memory_space=pltpu.SMEM)] + [hbm] * len(weights),
        out_specs=hbm,
        scratch_shapes=[
            v((rows, chans, cols), F32),
            v((rows, chans, cols), BF16),
            v((rows, chans, cols), F32),
            v((cols // LANES, chans * rows, LANES), F32),
            v((3, 6, chans, chans), BF16),
            v((3, 2, chans, LANES), F32),
            v((2, chans * rows, cols), BF16),
            v((2, chans * rows, cols), BF16),
            v((group0, own0, cols), BF16),
            v((group1, own1, cols), BF16),
            v((n_dev, own0, cols), BF16),
            v((n_dev, own1, cols), BF16),
            v((group0, own0, cols), BF16),
            v((group1, own1, cols), BF16),
            v((2, chans * rows, cols), BF16),
            v((heads * rows, cols), BF16),
            v((n_dev, heads * rows, cols), BF16),
            v((heads, cols, cols), F32),
            v((rows, chans, cols), BF16),
            v((rows, cols, chans), BF16),
            v((rows, chans, cols), BF16),
            v(early, F32),
            v((rows, cols, chans), F32),
            pltpu.SemaphoreType.DMA((phases, n_dev)),
            pltpu.SemaphoreType.DMA((phases, n_dev)),
            pltpu.SemaphoreType.DMA((1 + len(weights),)),
            pltpu.SemaphoreType.DMA((rows,)),
            v((rows, cols, chans), BF16),
            *[v(w.shape, w.dtype) for w in weights],
        ],
        compiler_params=pltpu.CompilerParams(
            collective_id=0, has_side_effects=True, vmem_limit_bytes=56 * 1024 * 1024
        ),
    )(pair_input, residue_mask.reshape(1, -1), residue_mask, *weights)


def solution(mesh):
    return jax.shard_map(
        functools.partial(shards, mesh.shape["row"]),
        mesh=mesh,
        in_specs=(P(("crop", "row"), None, None), P("crop")) + (P(),) * 17,
        out_specs=P(("crop", "row"), None, None),
        check_vma=False,
    )
```
